128 devices in a mesh: rows: 16 (over x, y), cols: 8 (over z, core).
Axes of the slice: x: 4, y: 4, z: 4, core: 2. Of those that a mesh axis runs over, the one named last changes fastest.
Arguments:
- guidance: float32 [3, 2048, 24576], P(None, 'rows', 'cols'), may hold values from -8 to 8
- initial: float32 [3, 2048, 24576], P(None, 'rows', 'cols'), may hold values from -6 to 6
- labels: int32 [2048, 24576], P('rows', 'cols'), may hold values from 0 to 5
- dirichlet: int32 [2048, 24576], P('rows', 'cols'), may hold values 0 or 1
Outputs:
- blended: float32 [3, 2048, 24576], P(None, 'rows', 'cols')
- residual: float32 [3, 2048, 24576], P(None, 'rows', 'cols')
The draws below stay inside these ranges and needn't reach their ends.
All inputs are finite; a program needn't handle non-finite values. No bound on the sum of `dirichlet` on one device may be relied on, other than what follows from the above.
Results may differ from the reference program's by a relative error of at most 0.0003.
Values sent between devices are 32-bit elements; how exact they have to be, the bound alone decides.
A program may use at most 128 MiB of HBM per device.

```python
import jax
import jax.numpy as jnp

CH = 3
ITERS = 3
NR = 2048
NC = 24576


def touch_ends(result, rng, least, largest):
    index_at = [jax.random.randint(jax.random.fold_in(rng, axis), (), 0, length) for axis, length in enumerate(result.shape)]
    widest = result.shape.index(max(result.shape))
    neighbour = index_at[:widest] + [(index_at[widest] + 1) % result.shape[widest]] + index_at[widest + 1:]
    return result.at[tuple(index_at)].set(least).at[tuple(neighbour)].set(largest)


def shard_levels(own_key, dims, split, least, top_value):
    level, own = 1.0, jax.random.fold_in(own_key, 6)
    for dim, shards_of in split:
        steps = jnp.exp(jax.random.uniform(jax.random.fold_in(own, dim), (shards_of,), jnp.float32, least / len(split), top_value / len(split)))
        level = level * jnp.repeat(steps, dims[dim] // shards_of).reshape([-1 if axis == dim else 1 for axis in range(len(dims))])
    return level


def noise(own_key, shape, deviation, reach, pieces=(), dtype=jnp.bfloat16):
    factor_of = shard_levels(own_key, shape, pieces, -0.22, 0.18) if pieces else 1.0
    values = jax.random.normal(own_key, shape, jnp.float32) * deviation * factor_of
    return jnp.minimum(jnp.maximum(values, -reach), reach).astype(dtype)


def setup_inputs(seed: int = 0) -> dict:
    key_of = jax.random.split(jax.random.key(seed), 5)
    guidance = noise(key_of[0], (CH, NR, NC), 1.0, 8.0, ((1, 16), (2, 8)), jnp.float32)
    initial = noise(key_of[1], (CH, NR, NC), 1.0, 6.0, ((1, 16), (2, 8)), jnp.float32)
    labels = touch_ends(jax.random.randint(key_of[2], (NR, NC), 0, 6), jax.random.fold_in(key_of[2], 1), 0, 5).astype(jnp.int32)
    dirichlet = touch_ends((jax.random.randint(key_of[3], (NR, NC), 0, 8) < 1).astype(jnp.int32), jax.random.fold_in(key_of[3], 1), 0, 1)
    return dict(guidance=guidance, initial=initial, labels=labels, dirichlet=dirichlet)


SCREEN = 0.1
SEAM_WEIGHT = 0.5


def edge_weights(labels):
    padded = jnp.pad(labels + 1, 1)
    center = padded[1:-1, 1:-1]
    sides = [padded[2:, 1:-1], padded[:-2, 1:-1], padded[1:-1, 2:], padded[1:-1, :-2]]
    return [jnp.where(side == center, 1.0, SEAM_WEIGHT).astype(jnp.float32) for side in sides]


def operate(field, weights):
    padded = jnp.pad(field, ((0, 0), (1, 1), (1, 1)))
    sides = [padded[:, 2:, 1:-1], padded[:, :-2, 1:-1], padded[:, 1:-1, 2:], padded[:, 1:-1, :-2]]
    total = SCREEN * field
    for weight, side in zip(weights, sides):
        total = total + weight * (field - side)
    return total


def reference(guidance, initial, labels, dirichlet):
    free_cells = (1 - dirichlet).astype(jnp.float32)
    weights = edge_weights(labels)
    residual = free_cells * (guidance - operate(initial, weights))
    blended = initial
    direction = residual
    norm_now = jnp.sum(residual * residual, axis=(1, 2))
    for turn_index in range(ITERS):
        applied = free_cells * operate(direction, weights)
        step_size = norm_now / jnp.sum(direction * applied, axis=(1, 2))
        blended = blended + step_size[:, None, None] * direction
        residual = residual - step_size[:, None, None] * applied
        norm_next = jnp.sum(residual * residual, axis=(1, 2))
        direction = residual + (norm_next / norm_now)[:, None, None] * direction
        norm_now = norm_next
    return blended, residual
```

```python
import functools

import jax
import jax.numpy as jnp
from jax import lax
from jax.experimental import pallas as pl
from jax.experimental.pallas import tpu as pltpu
from jax.sharding import PartitionSpec as P

ITERS = 3
CH = 3
SCREEN = 0.1
SEAM_WEIGHT = 0.5
SHIFT = 2.5
MESH = pl.DeviceIdType.MESH
BLOCK = 8


def neighbours(ref, lead, col, at, height, lane):
    here = ref[(*lead, col, pl.ds(at, height), slice(None))]
    up = ref[(*lead, col, pl.ds(at - 1, height), slice(None))]
    down = ref[(*lead, col, pl.ds(at + 1, height), slice(None))]
    before = ref[(*lead, col - 1, pl.ds(at, height), slice(None))]
    after = ref[(*lead, col + 1, pl.ds(at, height), slice(None))]
    axis = here.ndim - 1
    left = pltpu.roll(jnp.where(lane == 127, before, here), 1, axis)
    right = pltpu.roll(jnp.where(lane == 0, after, here), 127, axis)
    return here, down, up, right, left


def fold(values):
    parts = [values[:, at : at + 8] for at in range(0, values.shape[1], 8)]
    return functools.reduce(jnp.add, parts)


def krylov_kernel(
    guidance, initial, labels, dirichlet,
    x, u0, u1, u2, u3, coef,
    marks, fixed, weights, row_out, row_in, col_out, col_in, sums,
    gather_a, gather_b, mid, tile_sem, send_sem, recv_sem, a_send, a_recv, b_send, b_recv,
):
    n_rows, n_cols = lax.axis_size("rows"), lax.axis_size("cols")
    my_row, my_col = lax.axis_index("rows"), lax.axis_index("cols")
    rows, width = labels.shape
    tiles, steps = width // 128, rows // 8
    fields = (u0, u1, u2, u3)

    def columns(tile):
        return pl.ds(pl.multiple_of(tile * 128, 128), 128)

    def load_x(tile):
        return pltpu.make_async_copy(
            initial.at[:, :, columns(tile)], x.at[:, tile + 1, 8 : 8 + rows, :], tile_sem.at[2, tile]
        )

    def load_marks(tile):
        return pltpu.make_async_copy(
            labels.at[:, columns(tile)], marks.at[tile + 1, 8 : 8 + rows, :], tile_sem.at[3, tile]
        )

    def load_guidance(tile):
        return pltpu.make_async_copy(
            guidance.at[:, :, columns(tile)], u0.at[:, tile + 1, 8 : 8 + rows, :], tile_sem.at[0, tile]
        )

    def load_fixed(tile):
        return pltpu.make_async_copy(
            dirichlet.at[:, columns(tile)], fixed.at[tile + 1], tile_sem.at[1, tile]
        )

    @pl.loop(0, tiles)
    def _(tile):
        load_x(tile).start()
        load_marks(tile).start()

    @pl.loop(0, tiles)
    def _(tile):
        load_guidance(tile).start()
        load_fixed(tile).start()

    row_peers = [lax.rem(my_row + k, n_rows) for k in range(1, n_rows)]
    col_peers = [lax.rem(my_col + k, n_cols) for k in range(1, n_cols)]
    barrier = pltpu.get_barrier_semaphore()
    for peer in row_peers:
        pl.semaphore_signal(barrier, inc=1, device_id=(peer, my_col), device_id_type=MESH)
    for peer in col_peers:
        pl.semaphore_signal(barrier, inc=1, device_id=(my_row, peer), device_id_type=MESH)

    lane8 = lax.broadcasted_iota(jnp.int32, (8, 128), 1)
    row_up, row_down = lax.rem(my_row + n_rows - 1, n_rows), lax.rem(my_row + 1, n_rows)
    col_left, col_right = lax.rem(my_col + n_cols - 1, n_cols), lax.rem(my_col + 1, n_cols)

    def exchange(stage):
        count = (CH + 1) * tiles if stage == 0 else CH * tiles
        targets = ((row_up, my_col), (row_down, my_col), (my_row, col_left), (my_row, col_right))
        copies = []
        for way, target in enumerate(targets):
            if way < 2:
                src, dst = row_out.at[stage, way, 0:count], row_in.at[stage, way, 0:count]
            else:
                src, dst = col_out.at[stage, way - 2], col_in.at[stage, way - 2]
            copies.append(
                pltpu.make_async_remote_copy(
                    src_ref=src, dst_ref=dst, send_sem=send_sem.at[stage, way], recv_sem=recv_sem.at[stage, way],
                    device_id=target, device_id_type=MESH,
                )
            )
        return copies

    def send_rim(stage, field):
        @pl.loop(0, tiles)
        def _(tile):
            for way, at in ((0, 8), (1, 7 + rows)):
                for ch in range(CH):
                    row_out[stage, way, pl.ds(ch * tiles + tile, 1), :] = field[ch, tile + 1, at : at + 1, :]
                if stage == 0:
                    row_out[stage, way, pl.ds(CH * tiles + tile, 1), :] = marks[tile + 1, at : at + 1, :].astype(jnp.float32)

        for way, tile, lane in ((0, 1, 0), (1, tiles, 127)):
            packed = jnp.zeros((8, 128), jnp.float32)
            for step in range(steps):
                values = [field[ch, tile, 8 + step * 8 : 16 + step * 8, :] for ch in range(CH)]
                if stage == 0:
                    values.append(marks[tile, 8 + step * 8 : 16 + step * 8, :].astype(jnp.float32))
                for ch, value in enumerate(values):
                    place = ch * steps + step
                    packed = jnp.where(lane8 == place, pltpu.roll(value, (place - lane) % 128, 1), packed)
            col_out[stage, way] = packed
        for copy in exchange(stage):
            copy.start()

    def take_rim(stage, field):
        for copy in exchange(stage):
            copy.wait()
        above, below = my_row > 0, my_row < n_rows - 1

        @pl.loop(0, tiles)
        def _(tile):
            for way, at, there in ((1, 7, above), (0, 8 + rows, below)):
                for ch in range(CH):
                    value = row_in[stage, way, pl.ds(ch * tiles + tile, 1), :]
                    field[ch, tile + 1, at : at + 1, :] = jnp.where(there, value, 0.0)
                if stage == 0:
                    value = row_in[stage, way, pl.ds(CH * tiles + tile, 1), :].astype(jnp.int32)
                    marks[tile + 1, at : at + 1, :] = jnp.where(there, value, -1)

        for way, tile, lane, there in ((1, 0, 127, my_col > 0), (0, tiles + 1, 0, my_col < n_cols - 1)):
            packed = jnp.where(there, col_in[stage, way], 0.0)
            for step in range(steps):
                for ch in range(CH):
                    field[ch, tile, 8 + step * 8 : 16 + step * 8, :] = pltpu.roll(
                        packed, (lane - ch * steps - step) % 128, 1
                    )
            if stage == 0:
                packed = jnp.where(there, col_in[stage, way], -1.0)
                for step in range(steps):
                    marks[tile, 8 + step * 8 : 16 + step * 8, :] = pltpu.roll(
                        packed, (lane - CH * steps - step) % 128, 1
                    ).astype(jnp.int32)

    def first(tile, at, height, acc):
        lane = lax.broadcasted_iota(jnp.int32, (height, 128), 1)
        mark, *sides = neighbours(marks, (), tile, at, height, lane)
        free = (1 - fixed[tile, pl.ds(at - 8, height), :]).astype(jnp.float32)
        whole, part = -free, -SEAM_WEIGHT * free
        negated = [jnp.where(side == mark, whole, part) for side in sides]
        diagonal = SCREEN * free - ((negated[0] + negated[1]) + (negated[2] + negated[3]))
        for index, value in enumerate([diagonal - SHIFT * free, *negated]):
            weights[index, tile, pl.ds(at - 8, height), :] = value
        lane = lax.broadcasted_iota(jnp.int32, (CH, height, 128), 2)
        here, *sides = neighbours(x, (slice(None),), tile, at, height, lane)
        total = free * u0[:, tile, pl.ds(at, height), :] - diagonal * here
        for weight, side in zip(negated, sides):
            total = total - weight * side
        u0[:, tile, pl.ds(at, height), :] = total
        return (acc[0] + fold(total * total),)

    def apply(stage, tile, at, height, acc):
        source, target = fields[stage - 1], fields[stage]
        lane = lax.broadcasted_iota(jnp.int32, (CH, height, 128), 2)
        here, *sides = neighbours(source, (slice(None),), tile, at, height, lane)
        total = weights[0, tile, pl.ds(at - 8, height), :] * here
        for index, side in enumerate(sides):
            total = total + weights[index + 1, tile, pl.ds(at - 8, height), :] * side
        target[:, tile, pl.ds(at, height), :] = total
        cross = acc[0] + fold(here * total)
        if stage == ITERS:
            return (cross,)
        return (cross, acc[1] + fold(total * total))

    def work(stage, tile, at, height, acc):
        return first(tile, at, height, acc) if stage == 0 else apply(stage, tile, at, height, acc)

    def interior(stage):
        def body(tile, acc):
            if stage == 0:
                load_guidance(tile - 1).wait()
                load_fixed(tile - 1).wait()
            for at in range(16, rows, BLOCK):
                acc = work(stage, tile, at, BLOCK, acc)
            return acc

        return body

    def edge_rows(stage):
        def body(tile, acc):
            for at in (8, rows):
                acc = work(stage, tile, at, 8, acc)
            return acc

        return body

    def edge_columns(stage):
        def body(step, acc):
            for tile in (1, tiles):
                acc = work(stage, tile, pl.multiple_of(8 + step * 8, 8), 8, acc)
            return acc

        return body

    @pl.loop(0, tiles)
    def _(tile):
        load_x(tile).wait()
        load_marks(tile).wait()

    pl.semaphore_wait(barrier, n_rows - 1 + n_cols - 1)
    send_rim(0, x)
    for stage in range(ITERS + 1):
        acc = (jnp.zeros((CH, 8, 128), jnp.float32),) * (2 if 0 < stage < ITERS else 1)
        acc = lax.fori_loop(2, tiles, interior(stage), acc)
        take_rim(stage, x if stage == 0 else fields[stage - 1])
        if stage == 0:
            for tile in (0, tiles - 1):
                load_guidance(tile).wait()
                load_fixed(tile).wait()
        acc = lax.fori_loop(2, tiles, edge_rows(stage), acc)
        acc = lax.fori_loop(0, steps, edge_columns(stage), acc)
        if stage < ITERS:
            send_rim(stage + 1, fields[stage]) if stage + 1 <= ITERS else None
        for index, value in enumerate(acc):
            moment = 0 if stage == 0 else 2 * stage - 1 + index
            for ch in range(CH):
                sums[moment, ch : ch + 1, :] = jnp.sum(value[ch], axis=0, keepdims=True)

    message = jnp.zeros((8, 128), jnp.float32)
    in_use = lax.broadcasted_iota(jnp.int32, (8, 128), 0) < CH
    for moment in range(2 * ITERS):
        values = jnp.where(in_use, sums[moment], 0.0)
        message = jnp.where(lane8 == moment, jnp.sum(values, axis=1, keepdims=True), message)

    def all_gather(value, slots, mine, peers, index, send, recv):
        mine[...] = value
        copies = []
        for k, peer in enumerate(peers):
            copy = pltpu.make_async_remote_copy(
                src_ref=mine, dst_ref=slots.at[k], send_sem=send.at[k], recv_sem=recv.at[k],
                device_id=(peer, my_col) if index == 0 else (my_row, peer), device_id_type=MESH,
            )
            copy.start()
            copies.append(copy)
        for copy in copies:
            copy.wait()
        for k in range(len(peers)):
            value = value + slots[k]
        return value

    total = all_gather(message, gather_a, mid.at[0], col_peers, 1, a_send, a_recv)
    total = all_gather(total, gather_b, mid.at[1], row_peers, 0, b_send, b_recv)
    m = [jnp.broadcast_to(total[:, k : k + 1], (8, 128)) for k in range(2 * ITERS)]

    def dot(p, q, moments):
        return functools.reduce(
            jnp.add, [a * b * moments[i + j] for i, a in enumerate(p) for j, b in enumerate(q)]
        )

    image = [m[k + 1] + SHIFT * m[k] for k in range(2 * ITERS - 1)]
    one = jnp.ones((8, 128), jnp.float32)
    residual, direction, blended = [one], [one], []
    norm_now = m[0]
    for turn in range(ITERS):
        step_size = norm_now / dot(direction, direction, image)
        blended = [
            (blended[i] if i < len(blended) else 0.0) + step_size * p for i, p in enumerate(direction)
        ]
        applied = [SHIFT * p for p in direction] + [jnp.zeros_like(one)]
        for i, p in enumerate(direction):
            applied[i + 1] = applied[i + 1] + p
        residual = [
            (residual[i] if i < len(residual) else 0.0) - step_size * a for i, a in enumerate(applied)
        ]
        if turn + 1 < ITERS:
            norm_next = dot(residual, residual, m)
            ratio = norm_next / norm_now
            direction = [
                r + (ratio * direction[i] if i < len(direction) else 0.0) for i, r in enumerate(residual)
            ]
            norm_now = norm_next
    for index, value in enumerate(blended + residual):
        coef[index] = value


def combine_kernel(x, u0, u1, u2, u3, coef, blended, residual, stage, sem):
    rows = blended.shape[1]
    tiles = blended.shape[2] // 128

    def out(which, ref, tile):
        return pltpu.make_async_copy(
            stage.at[which, :, tile],
            ref.at[:, :, pl.ds(pl.multiple_of(tile * 128, 128), 128)],
            sem.at[which, tile],
        )

    @pl.loop(0, tiles)
    def _(tile):
        for ch in range(CH):
            c = [coef[i, ch : ch + 1, :] for i in range(2 * ITERS + 1)]
            for at in range(0, rows, BLOCK):
                here = pl.ds(8 + at, BLOCK)
                f = [u[ch, tile + 1, here, :] for u in (u0, u1, u2, u3)]
                iterate = x[ch, tile + 1, here, :] + c[0] * f[0] + c[1] * f[1] + c[2] * f[2]
                stage[0, ch, tile, at : at + BLOCK, :] = iterate
                stage[1, ch, tile, at : at + BLOCK, :] = (c[3] * f[0] + c[4] * f[1]) + (c[5] * f[2] + c[6] * f[3])
        out(0, blended, tile).start()
        out(1, residual, tile).start()

    @pl.loop(0, tiles)
    def _(tile):
        out(0, blended, tile).wait()
        out(1, residual, tile).wait()


def on_device(n_rows, n_cols, guidance, initial, labels, dirichlet):
    channels, rows, width = guidance.shape
    tiles = width // 128
    f32, i32 = jnp.float32, jnp.int32
    field = (channels, tiles + 2, rows + 16, 128)
    made_shape = pltpu.VMEM
    vmem, hbm = pl.BlockSpec(memory_space=pltpu.VMEM), pl.BlockSpec(memory_space=pltpu.HBM)
    arrays = [pltpu.with_memory_space_constraint(a, pltpu.HBM) for a in (guidance, initial, labels, dirichlet)]
    made = pl.pallas_call(
        krylov_kernel,
        out_shape=[made_shape(field, f32)] * 5 + [made_shape((2 * ITERS + 2, 8, 128), f32)],
        in_specs=[hbm] * 4,
        out_specs=[vmem] * 6,
        scratch_shapes=[
            pltpu.VMEM((tiles + 2, rows + 16, 128), i32),
            pltpu.VMEM((tiles + 2, rows, 128), i32),
            pltpu.VMEM((5, tiles + 2, rows, 128), f32),
            pltpu.VMEM((ITERS + 1, 2, (CH + 1) * tiles, 128), f32),
            pltpu.VMEM((ITERS + 1, 2, (CH + 1) * tiles, 128), f32),
            pltpu.VMEM((ITERS + 1, 2, 8, 128), f32),
            pltpu.VMEM((ITERS + 1, 2, 8, 128), f32),
            pltpu.VMEM((2 * ITERS, 8, 128), f32),
            pltpu.VMEM((n_cols - 1, 8, 128), f32),
            pltpu.VMEM((n_rows - 1, 8, 128), f32),
            pltpu.VMEM((2, 8, 128), f32),
            pltpu.SemaphoreType.DMA((4, tiles)),
            pltpu.SemaphoreType.DMA((ITERS + 1, 4)),
            pltpu.SemaphoreType.DMA((ITERS + 1, 4)),
            pltpu.SemaphoreType.DMA((n_cols - 1,)),
            pltpu.SemaphoreType.DMA((n_cols - 1,)),
            pltpu.SemaphoreType.DMA((n_rows - 1,)),
            pltpu.SemaphoreType.DMA((n_rows - 1,)),
        ],
        compiler_params=pltpu.CompilerParams(
            collective_id=0, has_side_effects=True, vmem_limit_bytes=20 * 2**20
        ),
    )(*arrays)
    made = [pltpu.with_memory_space_constraint(a, pltpu.VMEM) for a in made]
    blended, residual = pl.pallas_call(
        combine_kernel,
        out_shape=[jax.ShapeDtypeStruct(guidance.shape, f32)] * 2,
        in_specs=[vmem] * 6,
        out_specs=[hbm] * 2,
        scratch_shapes=[
            pltpu.VMEM((2, channels, tiles, rows, 128), f32),
            pltpu.SemaphoreType.DMA((2, tiles)),
        ],
        compiler_params=pltpu.CompilerParams(vmem_limit_bytes=12 * 2**20),
    )(*made)
    return blended, residual


def solution(mesh):
    s3, s2 = P(None, "rows", "cols"), P("rows", "cols")
    body = functools.partial(on_device, mesh.shape["rows"], mesh.shape["cols"])
    return jax.shard_map(
        body, mesh=mesh, in_specs=(s3, s3, s2, s2), out_specs=(s3, s3), check_vma=False
    )
```

```python
import functools

import jax
import jax.numpy as jnp
from jax import lax
from jax.experimental import pallas as pl
from jax.experimental.pallas import tpu as pltpu
from jax.sharding import PartitionSpec as P

ITERS = 3
CH = 3
SCREEN = 0.1
SEAM_WEIGHT = 0.5
SHIFT = 2.5
MESH = pl.DeviceIdType.MESH
GROUP = 11


def neighbours(ref, lead, col, at, height, lane):
    here = ref[(*lead, col, pl.ds(at, height), slice(None))]
    up = ref[(*lead, col, pl.ds(at - 1, height), slice(None))]
    down = ref[(*lead, col, pl.ds(at + 1, height), slice(None))]
    before = ref[(*lead, col - 1, pl.ds(at, height), slice(None))]
    after = ref[(*lead, col + 1, pl.ds(at, height), slice(None))]
    axis = here.ndim - 1
    left = pltpu.roll(jnp.where(lane == 127, before, here), 1, axis)
    right = pltpu.roll(jnp.where(lane == 0, after, here), 127, axis)
    return here, down, up, right, left


def group_of(tiles):
    return max(k for k in range(1, GROUP + 1) if (tiles - 2) % k == 0)


def krylov_kernel(
    guidance, initial, labels, dirichlet,
    x, u0, u1, u2, u3, coef,
    marks, fixed, weights, col_out, col_in, sums, gather_a, gather_b, mid,
    load_sem, tile_sem, send_sem, recv_sem, mark_sem, sum_sem,
):
    n_rows, n_cols = lax.axis_size("rows"), lax.axis_size("cols")
    my_row, my_col = lax.axis_index("rows"), lax.axis_index("cols")
    rows, width = labels.shape
    tiles, steps = width // 128, rows // 8
    fields = (u0, u1, u2, u3)
    group = group_of(tiles)
    groups = (tiles - 2) // group
    inside = pl.ds(8, rows)

    def columns(tile):
        return pl.ds(pl.multiple_of(tile * 128, 128), 128)

    def load(tile, of_x, of_marks):
        pltpu.make_async_copy(initial.at[:, :, columns(tile)], x.at[:, tile + 1, inside, :], of_x).start()
        pltpu.make_async_copy(labels.at[:, columns(tile)], marks.at[tile + 1, inside, :], of_marks).start()

    def load_later(tile, at):
        pltpu.make_async_copy(
            guidance.at[:, :, columns(tile)], u0.at[:, tile + 1, inside, :], tile_sem.at[0, at]
        ).start()
        pltpu.make_async_copy(dirichlet.at[:, columns(tile)], fixed.at[tile + 1], tile_sem.at[1, at]).start()

    def arrived(ref, sem):
        pltpu.make_async_copy(ref, ref, sem).wait()

    def arrived_later(first, count, at):
        arrived(u0.at[:, pl.ds(first + 1, count), inside, :], tile_sem.at[0, at])
        arrived(fixed.at[pl.ds(first + 1, count)], tile_sem.at[1, at])

    @pl.loop(0, tiles)
    def _(tile):
        load(tile, load_sem.at[0], load_sem.at[1])

    @pl.loop(0, groups)
    def _(at):
        @pl.loop(0, group)
        def _(k):
            load_later(1 + at * group + k, at)

    load_later(0, groups)
    load_later(tiles - 1, groups + 1)

    row_peers = [lax.rem(my_row + k, n_rows) for k in range(1, n_rows)]
    col_peers = [lax.rem(my_col + k, n_cols) for k in range(1, n_cols)]
    barrier = pltpu.get_barrier_semaphore()
    for peer in row_peers:
        pl.semaphore_signal(barrier, inc=1, device_id=(peer, my_col), device_id_type=MESH)
    for peer in col_peers:
        pl.semaphore_signal(barrier, inc=1, device_id=(my_row, peer), device_id_type=MESH)

    lane8 = lax.broadcasted_iota(jnp.int32, (8, 128), 1)
    row_up, row_down = lax.rem(my_row + n_rows - 1, n_rows), lax.rem(my_row + 1, n_rows)
    col_left, col_right = lax.rem(my_col + n_cols - 1, n_cols), lax.rem(my_col + 1, n_cols)
    not_first, not_last = my_row > 0, my_row < n_rows - 1
    middle = pl.ds(1, tiles)

    def clear(at):
        for k in range(1, tiles + 1):
            for ch in range(CH):
                for field in (x, u0, u1, u2):
                    field[ch, k, at : at + 8, :] = jnp.zeros((8, 128), jnp.float32)
            marks[k, at : at + 8, :] = jnp.full((8, 128), -1, jnp.int32)

    pl.when(jnp.logical_not(not_first))(lambda: clear(0))
    pl.when(jnp.logical_not(not_last))(lambda: clear(8 + rows))

    def row_copies(stage, field, upward):
        way = 0 if upward else 1
        source, target = (8, 8 + rows) if upward else (7 + rows, 7)
        peer = (row_up if upward else row_down, my_col)
        made = [
            pltpu.make_async_remote_copy(
                src_ref=field.at[:, middle, source : source + 1, :], dst_ref=field.at[:, middle, target : target + 1, :],
                send_sem=send_sem.at[way], recv_sem=recv_sem.at[stage % 2, way],
                device_id=peer, device_id_type=MESH,
            )
        ]
        if stage == 0:
            made.append(
                pltpu.make_async_remote_copy(
                    src_ref=marks.at[middle, source : source + 1, :], dst_ref=marks.at[middle, target : target + 1, :],
                    send_sem=mark_sem.at[0, way], recv_sem=mark_sem.at[1, way],
                    device_id=peer, device_id_type=MESH,
                )
            )
        return made

    def col_copies(stage):
        return [
            pltpu.make_async_remote_copy(
                src_ref=col_out.at[stage, side], dst_ref=col_in.at[stage, side],
                send_sem=send_sem.at[2 + side], recv_sem=recv_sem.at[stage % 2, 2 + side],
                device_id=(my_row, peer), device_id_type=MESH,
            )
            for side, peer in ((0, col_left), (1, col_right))
        ]

    def send_rim(stage, field):
        for upward, there in ((True, not_first), (False, not_last)):
            pl.when(there)(lambda upward=upward: [copy.start() for copy in row_copies(stage, field, upward)] and None)
        copies = col_copies(stage)
        for way, tile, lane in ((0, 1, 0), (1, tiles, 127)):
            packed = jnp.zeros((8, 128), jnp.float32)
            for step in range(steps):
                values = [field[ch, tile, 8 + step * 8 : 16 + step * 8, :] for ch in range(CH)]
                if stage == 0:
                    values.append(marks[tile, 8 + step * 8 : 16 + step * 8, :].astype(jnp.float32))
                for ch, value in enumerate(values):
                    place = ch * steps + step
                    packed = jnp.where(lane8 == place, pltpu.roll(value, (place - lane) % 128, 1), packed)
            col_out[stage, way] = packed
            copies[way].start()

    def take_rim(stage, field):
        for copy in col_copies(stage):
            copy.wait()
        for way, tile, lane, there in ((1, 0, 127, my_col > 0), (0, tiles + 1, 0, my_col < n_cols - 1)):
            packed = jnp.where(there, col_in[stage, way], 0.0)
            for step in range(steps):
                for ch in range(CH):
                    field[ch, tile, 8 + step * 8 : 16 + step * 8, :] = pltpu.roll(
                        packed, (lane - ch * steps - step) % 128, 1
                    )
            if stage == 0:
                packed = jnp.where(there, col_in[stage, way], -1.0)
                for step in range(steps):
                    marks[tile, 8 + step * 8 : 16 + step * 8, :] = pltpu.roll(
                        packed, (lane - CH * steps - step) % 128, 1
                    ).astype(jnp.int32)
        for upward, sent, came in ((True, not_first, not_last), (False, not_last, not_first)):
            pl.when(sent)(lambda upward=upward: [copy.wait_send() for copy in row_copies(stage, field, upward)] and None)
            pl.when(came)(lambda upward=upward: [copy.wait_recv() for copy in row_copies(stage, field, upward)] and None)

    def first(tile, at, acc):
        lane = lax.broadcasted_iota(jnp.int32, (8, 128), 1)
        mark, *sides = neighbours(marks, (), tile, at, 8, lane)
        free = (1 - fixed[tile, at - 8 : at, :]).astype(jnp.float32)
        whole, part = -free, -SEAM_WEIGHT * free
        negated = [jnp.where(side == mark, whole, part) for side in sides]
        diagonal = SCREEN * free - ((negated[0] + negated[1]) + (negated[2] + negated[3]))
        for index, value in enumerate([diagonal - SHIFT * free, *negated]):
            weights[index, tile, at - 8 : at, :] = value
        lane = lax.broadcasted_iota(jnp.int32, (CH, 8, 128), 2)
        here, *sides = neighbours(x, (slice(None),), tile, at, 8, lane)
        total = free * u0[:, tile, at : at + 8, :] - diagonal * here
        for weight, side in zip(negated, sides):
            total = total - weight * side
        u0[:, tile, at : at + 8, :] = total
        return (acc[0] + total * total,)

    def apply(stage, tile, at, acc):
        source, target = fields[stage - 1], fields[stage]
        lane = lax.broadcasted_iota(jnp.int32, (CH, 8, 128), 2)
        here, *sides = neighbours(source, (slice(None),), tile, at, 8, lane)
        total = weights[0, tile, at - 8 : at, :] * here
        for index, side in enumerate(sides):
            total = total + weights[index + 1, tile, at - 8 : at, :] * side
        target[:, tile, at : at + 8, :] = total
        cross = acc[0] + here * total
        if stage == ITERS:
            return (cross,)
        return (cross, acc[1] + total * total)

    def work(stage, tile, at, acc):
        return first(tile, at, acc) if stage == 0 else apply(stage, tile, at, acc)

    def interior(stage):
        def body(step, acc):
            if stage == 0:
                arrived_later(1 + step * group, group, step)
            for k in range(group):
                for at in range(16, rows, 8):
                    acc = work(stage, 2 + step * group + k, at, acc)
            return acc

        return body

    def edge_rows(stage):
        def body(step, acc):
            for k in range(EDGE_GROUP):
                for at in (8, rows):
                    acc = work(stage, 2 + step * EDGE_GROUP + k, at, acc)
            return acc

        return body

    EDGE_GROUP = max(k for k in range(1, 12) if (tiles - 2) % k == 0)

    arrived(x.at[:, middle, inside, :], load_sem.at[0])
    arrived(marks.at[middle, inside, :], load_sem.at[1])
    pl.semaphore_wait(barrier, n_rows - 1 + n_cols - 1)
    send_rim(0, x)
    for stage in range(ITERS + 1):
        acc = (jnp.zeros((CH, 8, 128), jnp.float32),) * (2 if 0 < stage < ITERS else 1)
        acc = lax.fori_loop(0, groups, interior(stage), acc)
        take_rim(stage, x if stage == 0 else fields[stage - 1])
        if stage == 0:
            arrived_later(0, 1, groups)
            arrived_later(tiles - 1, 1, groups + 1)
        acc = lax.fori_loop(0, (tiles - 2) // EDGE_GROUP, edge_rows(stage), acc)
        for tile in (1, tiles):
            for at in range(8, 8 + rows, 8):
                acc = work(stage, tile, at, acc)
        if stage < ITERS:
            send_rim(stage + 1, fields[stage])
        for index, value in enumerate(acc):
            moment = 0 if stage == 0 else 2 * stage - 1 + index
            for ch in range(CH):
                sums[moment, ch : ch + 1, :] = jnp.sum(value[ch], axis=0, keepdims=True)

    message = jnp.zeros((8, 128), jnp.float32)
    in_use = lax.broadcasted_iota(jnp.int32, (8, 128), 0) < CH
    for moment in range(2 * ITERS):
        values = jnp.where(in_use, sums[moment], 0.0)
        message = jnp.where(lane8 == moment, jnp.sum(values, axis=1, keepdims=True), message)

    def all_gather(value, slots, mine, peers, index):
        mine[...] = value
        for k, peer in enumerate(peers):
            pltpu.make_async_remote_copy(
                src_ref=mine, dst_ref=slots.at[k], send_sem=sum_sem.at[index, 0], recv_sem=sum_sem.at[index, 1],
                device_id=(peer, my_col) if index == 0 else (my_row, peer), device_id_type=MESH,
            ).start()
        arrived(slots, sum_sem.at[index, 1])
        arrived(slots, sum_sem.at[index, 0])
        for k in range(len(peers)):
            value = value + slots[k]
        return value

    total = all_gather(message, gather_a, mid.at[0], col_peers, 1)
    total = all_gather(total, gather_b, mid.at[1], row_peers, 0)
    m = [jnp.broadcast_to(total[:, k : k + 1], (8, 128)) for k in range(2 * ITERS)]

    def dot(p, q, moments):
        return functools.reduce(
            jnp.add, [a * b * moments[i + j] for i, a in enumerate(p) for j, b in enumerate(q)]
        )

    image = [m[k + 1] + SHIFT * m[k] for k in range(2 * ITERS - 1)]
    one = jnp.ones((8, 128), jnp.float32)
    residual, direction, blended = [one], [one], []
    norm_now = m[0]
    for turn in range(ITERS):
        step_size = norm_now / dot(direction, direction, image)
        blended = [
            (blended[i] if i < len(blended) else 0.0) + step_size * p for i, p in enumerate(direction)
        ]
        applied = [SHIFT * p for p in direction] + [jnp.zeros_like(one)]
        for i, p in enumerate(direction):
            applied[i + 1] = applied[i + 1] + p
        residual = [
            (residual[i] if i < len(residual) else 0.0) - step_size * a for i, a in enumerate(applied)
        ]
        if turn + 1 < ITERS:
            norm_next = dot(residual, residual, m)
            ratio = norm_next / norm_now
            direction = [
                r + (ratio * direction[i] if i < len(direction) else 0.0) for i, r in enumerate(residual)
            ]
            norm_now = norm_next
    for index, value in enumerate(blended + residual):
        coef[index] = value


def combine_kernel(x, u0, u1, u2, u3, coef, blended, residual, stage, sem):
    rows = blended.shape[1]
    tiles = blended.shape[2] // 128

    def out(which, ref, tile):
        return pltpu.make_async_copy(
            stage.at[which, :, tile],
            ref.at[:, :, pl.ds(pl.multiple_of(tile * 128, 128), 128)],
            sem.at[which, tile],
        )

    @pl.loop(0, tiles)
    def _(tile):
        for ch in range(CH):
            c = [coef[i, ch : ch + 1, :] for i in range(2 * ITERS + 1)]
            for at in range(0, rows, 8):
                here = pl.ds(8 + at, 8)
                f = [u[ch, tile + 1, here, :] for u in (u0, u1, u2, u3)]
                iterate = x[ch, tile + 1, here, :] + c[0] * f[0] + c[1] * f[1] + c[2] * f[2]
                stage[0, ch, tile, at : at + 8, :] = iterate
                stage[1, ch, tile, at : at + 8, :] = (c[3] * f[0] + c[4] * f[1]) + (c[5] * f[2] + c[6] * f[3])
        out(0, blended, tile).start()
        out(1, residual, tile).start()

    @pl.loop(0, tiles)
    def _(tile):
        out(0, blended, tile).wait()
        out(1, residual, tile).wait()


def on_device(n_rows, n_cols, guidance, initial, labels, dirichlet):
    channels, rows, width = guidance.shape
    tiles = width // 128
    f32, i32 = jnp.float32, jnp.int32
    field = (channels, tiles + 2, rows + 16, 128)
    made_shape = pltpu.VMEM
    vmem, hbm = pl.BlockSpec(memory_space=pltpu.VMEM), pl.BlockSpec(memory_space=pltpu.HBM)
    arrays = [pltpu.with_memory_space_constraint(a, pltpu.HBM) for a in (guidance, initial, labels, dirichlet)]
    made = pl.pallas_call(
        krylov_kernel,
        out_shape=[made_shape(field, f32)] * 5 + [made_shape((2 * ITERS + 2, 8, 128), f32)],
        in_specs=[hbm] * 4,
        out_specs=[vmem] * 6,
        scratch_shapes=[
            pltpu.VMEM((tiles + 2, rows + 16, 128), i32),
            pltpu.VMEM((tiles + 2, rows, 128), i32),
            pltpu.VMEM((5, tiles + 2, rows, 128), f32),
            pltpu.VMEM((ITERS + 1, 2, 8, 128), f32),
            pltpu.VMEM((ITERS + 1, 2, 8, 128), f32),
            pltpu.VMEM((2 * ITERS, 8, 128), f32),
            pltpu.VMEM((n_cols - 1, 8, 128), f32),
            pltpu.VMEM((n_rows - 1, 8, 128), f32),
            pltpu.VMEM((2, 8, 128), f32),
            pltpu.SemaphoreType.DMA((2,)),
            pltpu.SemaphoreType.DMA((2, (tiles - 2) // group_of(tiles) + 2)),
            pltpu.SemaphoreType.DMA((4,)),
            pltpu.SemaphoreType.DMA((2, 4)),
            pltpu.SemaphoreType.DMA((2, 2)),
            pltpu.SemaphoreType.DMA((2, 2)),
        ],
        compiler_params=pltpu.CompilerParams(
            collective_id=0, has_side_effects=True, vmem_limit_bytes=20 * 2**20
        ),
    )(*arrays)
    made = [pltpu.with_memory_space_constraint(a, pltpu.VMEM) for a in made]
    blended, residual = pl.pallas_call(
        combine_kernel,
        out_shape=[jax.ShapeDtypeStruct(guidance.shape, f32)] * 2,
        in_specs=[vmem] * 6,
        out_specs=[hbm] * 2,
        scratch_shapes=[
            pltpu.VMEM((2, channels, tiles, rows, 128), f32),
            pltpu.SemaphoreType.DMA((2, tiles)),
        ],
        compiler_params=pltpu.CompilerParams(vmem_limit_bytes=12 * 2**20),
    )(*made)
    return blended, residual


def solution(mesh):
    s3, s2 = P(None, "rows", "cols"), P("rows", "cols")
    body = functools.partial(on_device, mesh.shape["rows"], mesh.shape["cols"])
    return jax.shard_map(
        body, mesh=mesh, in_specs=(s3, s3, s2, s2), out_specs=(s3, s3), check_vma=False
    )
```

```python
import functools

import jax
import jax.numpy as jnp
from jax import lax
from jax.experimental import pallas as pl
from jax.experimental.pallas import tpu as pltpu
from jax.sharding import PartitionSpec as P

ITERS = 3
CH = 3
SCREEN = 0.1
SEAM_WEIGHT = 0.5
SHIFT = 2.5
MESH = pl.DeviceIdType.MESH
RIM = ITERS + 1
GROUP = 11


def neighbours(ref, lead, tile, at, lane):
    col, before, after = tile
    here = ref[(*lead, col, pl.ds(at, 8), slice(None))]
    up = ref[(*lead, col, pl.ds(at - 1, 8), slice(None))]
    down = ref[(*lead, col, pl.ds(at + 1, 8), slice(None))]
    axis = here.ndim - 1
    left = ref[(*lead, before, pl.ds(at, 8), slice(None))]
    right = ref[(*lead, after, pl.ds(at, 8), slice(None))]
    left = pltpu.roll(jnp.where(lane == 127, left, here), 1, axis)
    right = pltpu.roll(jnp.where(lane == 0, right, here), 127, axis)
    return here, down, up, right, left


PIECE = 4


def group_of(tiles):
    return max(k for k in range(1, GROUP + 1) if (tiles - 2) % k == 0)


def krylov_kernel(
    guidance, initial, labels, dirichlet,
    x, u0, u1, u2, u3, coef,
    marks, fixed, weights, col_out, col_in, sums, gather_a, gather_b, mid,
    load_sem, rim_sem, sum_sem,
):
    n_rows, n_cols = lax.axis_size("rows"), lax.axis_size("cols")
    my_row, my_col = lax.axis_index("rows"), lax.axis_index("cols")
    rows, width = labels.shape
    tiles = width // 128
    fields = (u0, u1, u2, u3)
    given = u3
    group = group_of(tiles)
    groups = (tiles - 2) // group
    inside, middle = pl.ds(8, rows), pl.ds(1, tiles)

    def load(tile, sem):
        columns = pl.ds(pl.multiple_of((tile - 1) * 128, 128), 128)
        pltpu.make_async_copy(initial.at[:, :, columns], x.at[:, tile, inside, :], sem).start()
        pltpu.make_async_copy(labels.at[:, columns], marks.at[tile, inside, :], sem).start()
        pltpu.make_async_copy(guidance.at[:, :, columns], given.at[:, tile, inside, :], sem).start()
        pltpu.make_async_copy(dirichlet.at[:, columns], fixed.at[tile, inside, :], sem).start()

    pieces = [(1, 2)]
    for start in range(0, tiles - 2, group):
        for k in range(0, group, PIECE):
            pieces.append((3 + start + k, min(PIECE, group - k)))
    for index, (tile, count) in enumerate(pieces):

        @pl.loop(tile, tile + count)
        def _(tile):
            load(tile, load_sem.at[index])

    row_peers = [lax.rem(my_row + k, n_rows) for k in range(1, n_rows)]
    col_peers = [lax.rem(my_col + k, n_cols) for k in range(1, n_cols)]
    row_up, row_down = row_peers[-1], row_peers[0]
    col_left, col_right = col_peers[-1], col_peers[0]
    diagonal_peers = [(r, c) for r in (row_up, row_down) for c in (col_left, col_right)]
    greeted = [(peer, my_col) for peer in row_peers] + [(my_row, peer) for peer in col_peers] + diagonal_peers
    barrier = pltpu.get_barrier_semaphore()
    for peer in greeted:
        pl.semaphore_signal(barrier, inc=1, device_id=peer, device_id_type=MESH)

    lane8 = lax.broadcasted_iota(jnp.int32, (8, 128), 1)
    sub8 = lax.broadcasted_iota(jnp.int32, (8, 128), 0)
    lane24 = lax.broadcasted_iota(jnp.int32, (CH, 8, 128), 2)
    every = (slice(None),)

    def arrived(ref, sem):
        pltpu.make_async_copy(ref, ref, sem).wait()

    def loaded(index):
        arrived(weights.at[0:4, pl.ds(1, 2 * pieces[index][1]), inside, :], load_sem.at[index])

    def remote(src, dst, send, recv, peer):
        return pltpu.make_async_remote_copy(
            src_ref=src, dst_ref=dst, send_sem=send, recv_sem=recv, device_id=peer, device_id_type=MESH
        )

    def rim_copies():
        copies = []
        for way, peer in ((0, row_up), (1, row_down)):
            for ref, size, lead in ((x, RIM, every), (given, RIM - 1, every), (marks, RIM, ()), (fixed, RIM - 1, ())):
                source, target = (8, 8 + rows) if way == 0 else (8 + rows - size, 8 - size)
                copies.append(
                    remote(
                        ref.at[(*lead, middle, pl.ds(source, size), slice(None))],
                        ref.at[(*lead, middle, pl.ds(target, size), slice(None))],
                        rim_sem.at[0, way], rim_sem.at[1, way], (peer, my_col),
                    )
                )
        for side, peer in ((0, col_left), (1, col_right)):
            for r, source, target, size in (
                (my_row, 8, 8, rows),
                (row_up, 8, 8 + rows, RIM),
                (row_down, 8 + rows - RIM, 8 - RIM, RIM),
            ):
                copies.append(
                    remote(
                        col_out.at[side, pl.ds(source, size)], col_in.at[side, pl.ds(target, size)],
                        rim_sem.at[0, 2 + side], rim_sem.at[1, 2 + side], (r, peer),
                    )
                )
        return copies

    def send_rim():
        for side, tile, lane in ((0, 1, 0), (1, tiles, 128 - RIM)):
            for at in range(8, 8 + rows, 8):
                values = [ref[ch, tile, at : at + 8, :] for ref in (x, given) for ch in range(CH)]
                values += [ref[tile, at : at + 8, :].astype(jnp.float32) for ref in (marks, fixed)]
                packed = jnp.zeros((8, 128), jnp.float32)
                for index, value in enumerate(values):
                    packed = jnp.where(lane8 // RIM == index, pltpu.roll(value, (index * RIM - lane) % 128, 1), packed)
                col_out[side, at : at + 8, :] = packed
        pl.semaphore_wait(barrier, len(greeted))
        for copy in rim_copies():
            copy.start()

    def take_rim():
        sent = (CH + 1) * (2 * RIM - 1)
        for kind in (1, 0):
            for way in range(2):
                arrived(marks.at[middle, pl.ds(0, sent), :], rim_sem.at[kind, way])
                arrived(col_in.at[way, pl.ds(8 - RIM, rows + 2 * RIM)], rim_sem.at[kind, 2 + way])
        blank = jnp.where(lane8 // RIM == 2 * CH, -1.0, jnp.where(lane8 // RIM == 2 * CH + 1, 1.0, 0.0))
        not_first, not_last = my_row > 0, my_row < n_rows - 1
        for at in range(0, 16 + rows, 8):
            there = [my_col < n_cols - 1, my_col > 0]
            if at == 0:
                there = [jnp.logical_and(t, not_first) for t in there]
            if at == 8 + rows:
                there = [jnp.logical_and(t, not_last) for t in there]
            right, left = [jnp.where(t, col_in[side, at : at + 8, :], blank) for side, t in enumerate(there)]
            for index in range(2 * CH + 2):
                value = jnp.where(
                    lane8 < 64,
                    pltpu.roll(right, (128 - index * RIM) % 128, 1),
                    pltpu.roll(left, (128 - RIM - index * RIM) % 128, 1),
                )
                if index < 2 * CH:
                    (x, given)[index // CH][index % CH, 0, at : at + 8, :] = value
                else:
                    (marks, fixed)[index - 2 * CH][0, at : at + 8, :] = value.astype(jnp.int32)

        def clear(at):
            for k in range(1, tiles + 1):
                for ref in (x, given):
                    ref[:, k, at : at + 8, :] = jnp.zeros((CH, 8, 128), jnp.float32)
                marks[k, at : at + 8, :] = jnp.full((8, 128), -1, jnp.int32)
                fixed[k, at : at + 8, :] = jnp.ones((8, 128), jnp.int32)

        pl.when(my_row == 0)(lambda: clear(0))
        pl.when(my_row == n_rows - 1)(lambda: clear(8 + rows))

    def first(tile, at):
        col, here8 = tile[0], pl.ds(at, 8)
        mark, *sides = neighbours(marks, (), tile, at, lane8)
        free = (1 - fixed[col, here8, :]).astype(jnp.float32)
        whole, part = -free, -SEAM_WEIGHT * free
        negated = [jnp.where(side == mark, whole, part) for side in sides]
        diagonal = SCREEN * free - ((negated[0] + negated[1]) + (negated[2] + negated[3]))
        for index, value in enumerate([diagonal - SHIFT * free, *negated]):
            weights[index, col, here8, :] = value
        here, *sides = neighbours(x, every, tile, at, lane24)
        total = free * given[:, col, here8, :] - diagonal * here
        for weight, side in zip(negated, sides):
            total = total - weight * side
        u0[:, col, here8, :] = total
        return None, total

    def work(stage, tile, at):
        if stage == 0:
            return first(tile, at)
        col, here8 = tile[0], pl.ds(at, 8)
        here, *sides = neighbours(fields[stage - 1], every, tile, at, lane24)
        total = weights[0, col, here8, :] * here
        for index, side in enumerate(sides):
            total = total + weights[index + 1, col, here8, :] * side
        fields[stage][:, col, here8, :] = total
        return here, total

    def inner(stage):
        low, high = 9 + stage, 8 + rows - 9 - stage
        last = stage == ITERS

        def body(step, acc):
            for k in range(group):
                if stage == 0 and step == 0 and k % PIECE == 0:
                    loaded(1 + k // PIECE)
                col = 2 + step * group + k
                tile = (col, col - 1, col + 1)
                if not last:
                    work(stage, tile, low)
                for at in range(16, rows, 8):
                    here, total = work(stage, tile, at)
                    products = [total * total] if stage == 0 else [here * total, total * total]
                    acc = tuple(a + p for a, p in zip(acc, products))
                if not last:
                    work(stage, tile, high)
            return acc

        acc = (jnp.zeros((CH, 8, 128), jnp.float32),) * (2 if 0 < stage < ITERS else 1)
        if stage == 0:
            loaded(0)
            acc = body(0, acc)
            for index in range(1 + -(-group // PIECE), len(pieces)):
                loaded(index)
            send_rim()
            for step in range(1, groups):
                acc = body(step, acc)
        else:
            acc = lax.fori_loop(0, groups, body, acc)
        if not last:
            for tile in ((1, 1, 2), (tiles, tiles - 1, tiles)):
                for at in (low, *range(16, rows, 8), high):
                    work(stage, tile, at)
        return acc

    def outer(stage):
        beyond = RIM - 1 - stage
        low, high = 8 - beyond, rows + beyond
        last = stage == ITERS

        def products(tile, at, acc):
            here, total = work(stage, tile, at)
            if not last:
                return acc
            zero, one = [field[:, tile[0], pl.ds(at, 8), :] for field in (u0, u1)]
            pairs = [(zero, zero), (zero, one), (one, one), (one, here), (here, here), (here, total)]
            return tuple(a + p * q for a, (p, q) in zip(acc, pairs))

        acc = (jnp.zeros((CH, 8, 128), jnp.float32),) * (2 * ITERS if last else 0)
        for col in range(2, tiles):
            for at in (low, high):
                acc = products((col, col - 1, col + 1), at, acc)
        around = [(1, 0, 2), (tiles, tiles - 1, 0)] + ([] if last else [(0, tiles, 1)])
        for tile in around:
            for at in (*(() if last else (low, high)), *range(8, 8 + rows, 8)):
                acc = products(tile, at, acc)
        return acc

    moments = []
    for stage in range(ITERS + 1):
        moments.extend(inner(stage))
    take_rim()
    for stage in range(ITERS):
        outer(stage)
    moments = [a + b for a, b in zip(moments, outer(ITERS))]

    message = jnp.zeros((8, 128), jnp.float32)
    for index, value in enumerate(moments):
        for ch in range(CH):
            sums[index, ch : ch + 1, :] = jnp.sum(value[ch], axis=0, keepdims=True)
        total = jnp.sum(jnp.where(sub8 < CH, sums[index], 0.0), axis=1, keepdims=True)
        message = jnp.where(lane8 == 8 * index + sub8, total, message)
    message = jnp.sum(message, axis=0, keepdims=True)

    def add_up(value, slots, mine, peers, index):
        mine[...] = value
        for k, peer in enumerate(peers):
            target = (peer, my_col) if index == 0 else (my_row, peer)
            remote(mine, slots.at[k], sum_sem.at[index, 0], sum_sem.at[index, 1], target).start()
        arrived(slots, sum_sem.at[index, 1])
        arrived(slots, sum_sem.at[index, 0])
        parts = [value] + [slots[k] for k in range(len(peers))]
        while len(parts) > 1:
            parts = [functools.reduce(jnp.add, parts[i : i + 2]) for i in range(0, len(parts), 2)]
        return parts[0]

    total = add_up(message, gather_a, mid.at[0], col_peers, 1)
    total = jnp.broadcast_to(add_up(total, gather_b, mid.at[1], row_peers, 0), (8, 128))
    m = [
        jnp.broadcast_to(jnp.sum(jnp.where(lane8 == 8 * k + sub8, total, 0.0), axis=1, keepdims=True), (8, 128))
        for k in range(2 * ITERS)
    ]

    def dot(p, q, moments):
        return functools.reduce(
            jnp.add, [a * b * moments[i + j] for i, a in enumerate(p) for j, b in enumerate(q)]
        )

    image = [m[k + 1] + SHIFT * m[k] for k in range(2 * ITERS - 1)]
    one = jnp.ones((8, 128), jnp.float32)
    residual, direction, blended = [one], [one], []
    norm_now = m[0]
    for turn in range(ITERS):
        step_size = norm_now / dot(direction, direction, image)
        blended = [
            (blended[i] if i < len(blended) else 0.0) + step_size * p for i, p in enumerate(direction)
        ]
        applied = [SHIFT * p for p in direction] + [jnp.zeros_like(one)]
        for i, p in enumerate(direction):
            applied[i + 1] = applied[i + 1] + p
        residual = [
            (residual[i] if i < len(residual) else 0.0) - step_size * a for i, a in enumerate(applied)
        ]
        if turn + 1 < ITERS:
            norm_next = dot(residual, residual, m)
            ratio = norm_next / norm_now
            direction = [
                r + (ratio * direction[i] if i < len(direction) else 0.0) for i, r in enumerate(residual)
            ]
            norm_now = norm_next
    for index, value in enumerate(blended + residual):
        coef[index] = value


def combine_kernel(x, u0, u1, u2, u3, coef, blended, residual, stage, sem):
    rows = blended.shape[1]
    tiles = blended.shape[2] // 128

    def out(which, ref, step):
        here = pl.ds(pl.multiple_of(step * 8, 8), 8)
        return pltpu.make_async_copy(stage.at[which, :, here], ref.at[:, here], sem.at[which])

    @pl.loop(0, rows // 8)
    def _(step):
        there = pl.ds(pl.multiple_of(step * 8, 8), 8)
        here = pl.ds(pl.multiple_of(8 + step * 8, 8), 8)
        for ch in range(CH):
            c = [coef[i, ch : ch + 1, :] for i in range(2 * ITERS + 1)]
            for tile in range(tiles):
                f = [u[ch, tile + 1, here, :] for u in (u0, u1, u2, u3)]
                iterate = x[ch, tile + 1, here, :] + c[0] * f[0] + c[1] * f[1] + c[2] * f[2]
                columns = slice(tile * 128, tile * 128 + 128)
                stage[0, ch, there, columns] = iterate
                stage[1, ch, there, columns] = (c[3] * f[0] + c[4] * f[1]) + (c[5] * f[2] + c[6] * f[3])
        out(0, blended, step).start()
        out(1, residual, step).start()

    for which, ref in enumerate((blended, residual)):
        pltpu.make_async_copy(stage.at[which], ref, sem.at[which]).wait()


def on_device(n_rows, n_cols, guidance, initial, labels, dirichlet):
    channels, rows, width = guidance.shape
    tiles = width // 128
    f32, i32 = jnp.float32, jnp.int32
    plane = (tiles + 1, rows + 16, 128)
    field = (channels, *plane)
    made_shape = pltpu.VMEM
    vmem, hbm = pl.BlockSpec(memory_space=pltpu.VMEM), pl.BlockSpec(memory_space=pltpu.HBM)
    arrays = [pltpu.with_memory_space_constraint(a, pltpu.HBM) for a in (guidance, initial, labels, dirichlet)]
    made = pl.pallas_call(
        krylov_kernel,
        out_shape=[made_shape(field, f32)] * 5 + [made_shape((2 * ITERS + 2, 8, 128), f32)],
        in_specs=[hbm] * 4,
        out_specs=[vmem] * 6,
        scratch_shapes=[
            pltpu.VMEM(plane, i32),
            pltpu.VMEM(plane, i32),
            pltpu.VMEM((5, *plane), f32),
            pltpu.VMEM((2, rows + 16, 128), f32),
            pltpu.VMEM((2, rows + 16, 128), f32),
            pltpu.VMEM((2 * ITERS, 8, 128), f32),
            pltpu.VMEM((n_cols - 1, 1, 128), f32),
            pltpu.VMEM((n_rows - 1, 1, 128), f32),
            pltpu.VMEM((2, 1, 128), f32),
            pltpu.SemaphoreType.DMA((1 + (tiles - 2) // group_of(tiles) * -(-group_of(tiles) // PIECE),)),
            pltpu.SemaphoreType.DMA((2, 4)),
            pltpu.SemaphoreType.DMA((2, 2)),
        ],
        compiler_params=pltpu.CompilerParams(
            collective_id=0, has_side_effects=True, vmem_limit_bytes=20 * 2**20
        ),
    )(*arrays)
    made = [pltpu.with_memory_space_constraint(a, pltpu.VMEM) for a in made]
    blended, residual = pl.pallas_call(
        combine_kernel,
        out_shape=[jax.ShapeDtypeStruct(guidance.shape, f32)] * 2,
        in_specs=[vmem] * 6,
        out_specs=[hbm] * 2,
        scratch_shapes=[
            pltpu.VMEM((2, channels, rows, width), f32),
            pltpu.SemaphoreType.DMA((2,)),
        ],
        compiler_params=pltpu.CompilerParams(vmem_limit_bytes=12 * 2**20),
    )(*made)
    return blended, residual


def solution(mesh):
    s3, s2 = P(None, "rows", "cols"), P("rows", "cols")
    body = functools.partial(on_device, mesh.shape["rows"], mesh.shape["cols"])
    return jax.shard_map(
        body, mesh=mesh, in_specs=(s3, s3, s2, s2), out_specs=(s3, s3), check_vma=False
    )
```

```python
import functools

import jax
import jax.numpy as jnp
from jax import lax
from jax.experimental import pallas as pl
from jax.experimental.pallas import tpu as pltpu
from jax.sharding import PartitionSpec as P

ITERS = 3
CH = 3
SCREEN = 0.1
SEAM_WEIGHT = 0.5
SHIFT = 2.5
MESH = pl.DeviceIdType.MESH
RIM = ITERS + 1
GROUP = 11


def neighbours(ref, lead, tile, at, lane):
    col, before, after = tile
    here = ref[(*lead, col, pl.ds(at, 8), slice(None))]
    up = ref[(*lead, col, pl.ds(at - 1, 8), slice(None))]
    down = ref[(*lead, col, pl.ds(at + 1, 8), slice(None))]
    axis = here.ndim - 1
    left = ref[(*lead, before, pl.ds(at, 8), slice(None))]
    right = ref[(*lead, after, pl.ds(at, 8), slice(None))]
    left = pltpu.roll(jnp.where(lane == 127, left, here), 1, axis)
    right = pltpu.roll(jnp.where(lane == 0, right, here), 127, axis)
    return here, down, up, right, left


PIECE = 4


def group_of(tiles):
    return max(k for k in range(1, GROUP + 1) if (tiles - 2) % k == 0)


def krylov_kernel(
    guidance, initial, labels, dirichlet,
    x, u0, u1, u2, u3, coef,
    marks, fixed, weights, col_out, col_in, sums, gather_a, gather_b, mine,
    load_sem, rim_sem, sum_sem,
):
    n_rows, n_cols = lax.axis_size("rows"), lax.axis_size("cols")
    my_row, my_col = lax.axis_index("rows"), lax.axis_index("cols")
    rows, width = labels.shape
    tiles = width // 128
    fields = (u0, u1, u2, u3)
    given = u3
    group = group_of(tiles)
    groups = (tiles - 2) // group
    inside, middle = pl.ds(8, rows), pl.ds(1, tiles)

    def load(tile, sem):
        columns = pl.ds(pl.multiple_of((tile - 1) * 128, 128), 128)
        pltpu.make_async_copy(initial.at[:, :, columns], x.at[:, tile, inside, :], sem).start()
        pltpu.make_async_copy(labels.at[:, columns], marks.at[tile, inside, :], sem).start()
        pltpu.make_async_copy(guidance.at[:, :, columns], given.at[:, tile, inside, :], sem).start()
        pltpu.make_async_copy(dirichlet.at[:, columns], fixed.at[tile, inside, :], sem).start()

    pieces = [(1, 2)]
    for start in range(0, tiles - 2, group):
        for k in range(0, group, PIECE):
            pieces.append((3 + start + k, min(PIECE, group - k)))
    for index, (tile, count) in enumerate(pieces):

        @pl.loop(tile, tile + count)
        def _(tile):
            load(tile, load_sem.at[index])

    row_peers = [lax.rem(my_row + k, n_rows) for k in range(1, n_rows)]
    col_peers = [lax.rem(my_col + k, n_cols) for k in range(1, n_cols)]
    row_up, row_down = row_peers[-1], row_peers[0]
    col_left, col_right = col_peers[-1], col_peers[0]
    diagonal_peers = [(r, c) for r in (row_up, row_down) for c in (col_left, col_right)]
    greeted = [(peer, my_col) for peer in row_peers] + [(my_row, peer) for peer in col_peers] + diagonal_peers
    barrier = pltpu.get_barrier_semaphore()
    for peer in greeted:
        pl.semaphore_signal(barrier, inc=1, device_id=peer, device_id_type=MESH)

    lane8 = lax.broadcasted_iota(jnp.int32, (8, 128), 1)
    sub8 = lax.broadcasted_iota(jnp.int32, (8, 128), 0)
    lane24 = lax.broadcasted_iota(jnp.int32, (CH, 8, 128), 2)
    every = (slice(None),)

    def arrived(ref, sem):
        pltpu.make_async_copy(ref, ref, sem).wait()

    def loaded(index):
        arrived(weights.at[0:4, pl.ds(1, 2 * pieces[index][1]), inside, :], load_sem.at[index])

    def remote(src, dst, send, recv, peer):
        return pltpu.make_async_remote_copy(
            src_ref=src, dst_ref=dst, send_sem=send, recv_sem=recv, device_id=peer, device_id_type=MESH
        )

    def rim_copies():
        copies = []
        for way, peer in ((0, row_up), (1, row_down)):
            for ref, size, lead in ((x, RIM, every), (given, RIM - 1, every), (marks, RIM, ()), (fixed, RIM - 1, ())):
                source, target = (8, 8 + rows) if way == 0 else (8 + rows - size, 8 - size)
                copies.append(
                    remote(
                        ref.at[(*lead, middle, pl.ds(source, size), slice(None))],
                        ref.at[(*lead, middle, pl.ds(target, size), slice(None))],
                        rim_sem.at[0, way], rim_sem.at[1, way], (peer, my_col),
                    )
                )
        for side, peer in ((0, col_left), (1, col_right)):
            for r, source, target, size in (
                (my_row, 8, 8, rows),
                (row_up, 8, 8 + rows, RIM),
                (row_down, 8 + rows - RIM, 8 - RIM, RIM),
            ):
                copies.append(
                    remote(
                        col_out.at[side, pl.ds(source, size)], col_in.at[side, pl.ds(target, size)],
                        rim_sem.at[0, 2 + side], rim_sem.at[1, 2 + side], (r, peer),
                    )
                )
        return copies

    def send_rim():
        for side, tile, lane in ((0, 1, 0), (1, tiles, 128 - RIM)):
            for at in range(8, 8 + rows, 8):
                values = [ref[ch, tile, at : at + 8, :] for ref in (x, given) for ch in range(CH)]
                values += [ref[tile, at : at + 8, :].astype(jnp.float32) for ref in (marks, fixed)]
                packed = jnp.zeros((8, 128), jnp.float32)
                for index, value in enumerate(values):
                    packed = jnp.where(lane8 // RIM == index, pltpu.roll(value, (index * RIM - lane) % 128, 1), packed)
                col_out[side, at : at + 8, :] = packed
        pl.semaphore_wait(barrier, len(greeted))
        for copy in rim_copies():
            copy.start()

    def take_rim():
        sent = (CH + 1) * (2 * RIM - 1)
        for kind in (1, 0):
            for way in range(2):
                arrived(marks.at[middle, pl.ds(0, sent), :], rim_sem.at[kind, way])
                arrived(col_in.at[way, pl.ds(8 - RIM, rows + 2 * RIM)], rim_sem.at[kind, 2 + way])
        blank = jnp.where(lane8 // RIM == 2 * CH, -1.0, jnp.where(lane8 // RIM == 2 * CH + 1, 1.0, 0.0))
        not_first, not_last = my_row > 0, my_row < n_rows - 1
        for at in range(0, 16 + rows, 8):
            there = [my_col < n_cols - 1, my_col > 0]
            if at == 0:
                there = [jnp.logical_and(t, not_first) for t in there]
            if at == 8 + rows:
                there = [jnp.logical_and(t, not_last) for t in there]
            right, left = [jnp.where(t, col_in[side, at : at + 8, :], blank) for side, t in enumerate(there)]
            for index in range(2 * CH + 2):
                value = jnp.where(
                    lane8 < 64,
                    pltpu.roll(right, (128 - index * RIM) % 128, 1),
                    pltpu.roll(left, (128 - RIM - index * RIM) % 128, 1),
                )
                if index < 2 * CH:
                    (x, given)[index // CH][index % CH, 0, at : at + 8, :] = value
                else:
                    (marks, fixed)[index - 2 * CH][0, at : at + 8, :] = value.astype(jnp.int32)

        def clear(at):
            for k in range(1, tiles + 1):
                for ref in (x, given):
                    ref[:, k, at : at + 8, :] = jnp.zeros((CH, 8, 128), jnp.float32)
                marks[k, at : at + 8, :] = jnp.full((8, 128), -1, jnp.int32)
                fixed[k, at : at + 8, :] = jnp.ones((8, 128), jnp.int32)

        pl.when(my_row == 0)(lambda: clear(0))
        pl.when(my_row == n_rows - 1)(lambda: clear(8 + rows))

    def first(tile, at):
        col, here8 = tile[0], pl.ds(at, 8)
        mark, *sides = neighbours(marks, (), tile, at, lane8)
        free = (1 - fixed[col, here8, :]).astype(jnp.float32)
        whole, part = -free, -SEAM_WEIGHT * free
        negated = [jnp.where(side == mark, whole, part) for side in sides]
        diagonal = SCREEN * free - ((negated[0] + negated[1]) + (negated[2] + negated[3]))
        for index, value in enumerate([diagonal - SHIFT * free, *negated]):
            weights[index, col, here8, :] = value
        here, *sides = neighbours(x, every, tile, at, lane24)
        total = free * given[:, col, here8, :] - diagonal * here
        for weight, side in zip(negated, sides):
            total = total - weight * side
        u0[:, col, here8, :] = total
        return None, total

    def work(stage, tile, at):
        if stage == 0:
            return first(tile, at)
        col, here8 = tile[0], pl.ds(at, 8)
        here, *sides = neighbours(fields[stage - 1], every, tile, at, lane24)
        total = weights[0, col, here8, :] * here
        for index, side in enumerate(sides):
            total = total + weights[index + 1, col, here8, :] * side
        fields[stage][:, col, here8, :] = total
        return here, total

    def form(tile, at):
        col, _, after = tile
        here8 = pl.ds(at, 8)
        here = u2[:, col, here8, :]
        right = pltpu.roll(jnp.where(lane24 == 0, u2[:, after, here8, :], here), 127, 2)
        own = weights[0, col, here8, :] * here
        edges = weights[1, col, here8, :] * u2[:, col, pl.ds(at + 1, 8), :] + weights[3, col, here8, :] * right
        return here, here * own, here * edges

    def add(acc, products):
        return tuple(a + p for a, p in zip(acc, products))

    def inner(stage):
        low, high = 9 + stage, 8 + rows - 9 - stage
        last = stage == ITERS

        def body(step, acc):
            for k in range(group):
                if stage == 0 and step == 0 and k % PIECE == 0:
                    loaded(1 + k // PIECE)
                col = 2 + step * group + k
                tile = (col, col - 1, col + 1)
                if not last:
                    work(stage, tile, low)
                for at in range(16, rows, 8):
                    if last:
                        acc = add(acc, form(tile, at)[1:])
                        continue
                    here, total = work(stage, tile, at)
                    acc = add(acc, [total * total] if stage == 0 else [here * total, total * total])
                if not last:
                    work(stage, tile, high)
            return acc

        acc = (jnp.zeros((CH, 8, 128), jnp.float32),) * (1 if stage == 0 else 2)
        if stage == 0:
            loaded(0)
            acc = body(0, acc)
            for index in range(1 + -(-group // PIECE), len(pieces)):
                loaded(index)
            send_rim()
            for step in range(1, groups):
                acc = body(step, acc)
        else:
            acc = lax.fori_loop(0, groups, body, acc)
        if not last:
            for tile in ((1, 1, 2), (tiles, tiles - 1, tiles)):
                for at in (low, *range(16, rows, 8), high):
                    work(stage, tile, at)
        return acc

    sides = [(1, 0, 2), (tiles, tiles - 1, 0)]

    def outer(stage):
        beyond = RIM - 1 - stage
        low, high = 8 - beyond, rows + beyond
        for col in range(2, tiles):
            for at in (low, high):
                work(stage, (col, col - 1, col + 1), at)
        for tile in (*sides, (0, tiles, 1)):
            for at in (low, *range(8, 8 + rows, 8), high):
                work(stage, tile, at)

    def outer_sums(acc):
        places = [((col, col - 1, col + 1), at) for col in range(2, tiles) for at in (8, rows)]
        places += [(tile, at) for tile in sides for at in range(8, 8 + rows, 8)]
        for tile, at in places:
            zero, one = [field[:, tile[0], pl.ds(at, 8), :] for field in (u0, u1)]
            two, own, edges = form(tile, at)
            acc = add(acc, [zero * zero, zero * one, one * one, one * two, two * two, own, edges])
        return acc

    def final_stage(part):
        def body(step, carry):
            for k in range(group):
                col = 2 + step * group + k
                for at in range(8, 8 + rows, 8):
                    work(ITERS, (col, col - 1, col + 1), at)
            return carry

        half = groups // 2
        lax.fori_loop(half * part, groups if part else half, body, 0)
        for at in range(8, 8 + rows, 8):
            work(ITERS, sides[part], at)

    moments = []
    for stage in range(ITERS + 1):
        moments.extend(inner(stage))
    take_rim()
    for stage in range(ITERS):
        outer(stage)
    *moments, own, edges = outer_sums(moments)
    moments.append(own + 2.0 * edges)

    message = jnp.zeros((8, 128), jnp.float32)
    for index, value in enumerate(moments):
        for ch in range(CH):
            sums[index, ch : ch + 1, :] = jnp.sum(value[ch], axis=0, keepdims=True)
        total = jnp.sum(jnp.where(sub8 < CH, sums[index], 0.0), axis=1, keepdims=True)
        message = jnp.where(lane8 == 8 * index + sub8, total, message)
    message = jnp.sum(message, axis=0, keepdims=True)

    total = message
    for part, (slots, targets) in enumerate(
        ((gather_a, [(my_row, peer) for peer in col_peers]), (gather_b, [(peer, my_col) for peer in row_peers]))
    ):
        mine[part] = total
        for k, target in enumerate(targets):
            remote(mine.at[part], slots.at[k], sum_sem.at[part, 0], sum_sem.at[part, 1], target).start()
        final_stage(part)
        arrived(slots, sum_sem.at[part, 1])
        arrived(slots, sum_sem.at[part, 0])
        parts = [total] + [slots[k] for k in range(len(targets))]
        while len(parts) > 1:
            parts = [functools.reduce(jnp.add, parts[i : i + 2]) for i in range(0, len(parts), 2)]
        total = parts[0]
    total = jnp.broadcast_to(total, (8, 128))
    m = [
        jnp.broadcast_to(jnp.sum(jnp.where(lane8 == 8 * k + sub8, total, 0.0), axis=1, keepdims=True), (8, 128))
        for k in range(2 * ITERS)
    ]

    def dot(p, q, moments):
        return functools.reduce(
            jnp.add, [a * b * moments[i + j] for i, a in enumerate(p) for j, b in enumerate(q)]
        )

    image = [m[k + 1] + SHIFT * m[k] for k in range(2 * ITERS - 1)]
    one = jnp.ones((8, 128), jnp.float32)
    residual, direction, blended = [one], [one], []
    norm_now = m[0]
    for turn in range(ITERS):
        step_size = norm_now / dot(direction, direction, image)
        blended = [
            (blended[i] if i < len(blended) else 0.0) + step_size * p for i, p in enumerate(direction)
        ]
        applied = [SHIFT * p for p in direction] + [jnp.zeros_like(one)]
        for i, p in enumerate(direction):
            applied[i + 1] = applied[i + 1] + p
        residual = [
            (residual[i] if i < len(residual) else 0.0) - step_size * a for i, a in enumerate(applied)
        ]
        if turn + 1 < ITERS:
            norm_next = dot(residual, residual, m)
            ratio = norm_next / norm_now
            direction = [
                r + (ratio * direction[i] if i < len(direction) else 0.0) for i, r in enumerate(residual)
            ]
            norm_now = norm_next
    for index, value in enumerate(blended + residual):
        coef[index] = value


def combine_kernel(x, u0, u1, u2, u3, coef, blended, residual, stage, sem):
    rows = blended.shape[1]
    tiles = blended.shape[2] // 128

    def out(which, ref, step):
        here = pl.ds(pl.multiple_of(step * 8, 8), 8)
        return pltpu.make_async_copy(stage.at[which, :, here], ref.at[:, here], sem.at[which])

    @pl.loop(0, rows // 8)
    def _(step):
        there = pl.ds(pl.multiple_of(step * 8, 8), 8)
        here = pl.ds(pl.multiple_of(8 + step * 8, 8), 8)
        for ch in range(CH):
            c = [coef[i, ch : ch + 1, :] for i in range(2 * ITERS + 1)]
            for tile in range(tiles):
                f = [u[ch, tile + 1, here, :] for u in (u0, u1, u2, u3)]
                iterate = x[ch, tile + 1, here, :] + c[0] * f[0] + c[1] * f[1] + c[2] * f[2]
                columns = slice(tile * 128, tile * 128 + 128)
                stage[0, ch, there, columns] = iterate
                stage[1, ch, there, columns] = (c[3] * f[0] + c[4] * f[1]) + (c[5] * f[2] + c[6] * f[3])
        out(0, blended, step).start()
        out(1, residual, step).start()

    for which, ref in enumerate((blended, residual)):
        pltpu.make_async_copy(stage.at[which], ref, sem.at[which]).wait()


def on_device(n_rows, n_cols, guidance, initial, labels, dirichlet):
    channels, rows, width = guidance.shape
    tiles = width // 128
    f32, i32 = jnp.float32, jnp.int32
    plane = (tiles + 1, rows + 16, 128)
    field = (channels, *plane)
    made_shape = pltpu.VMEM
    vmem, hbm = pl.BlockSpec(memory_space=pltpu.VMEM), pl.BlockSpec(memory_space=pltpu.HBM)
    arrays = [pltpu.with_memory_space_constraint(a, pltpu.HBM) for a in (guidance, initial, labels, dirichlet)]
    made = pl.pallas_call(
        krylov_kernel,
        out_shape=[made_shape(field, f32)] * 5 + [made_shape((2 * ITERS + 2, 8, 128), f32)],
        in_specs=[hbm] * 4,
        out_specs=[vmem] * 6,
        scratch_shapes=[
            pltpu.VMEM(plane, i32),
            pltpu.VMEM(plane, i32),
            pltpu.VMEM((5, *plane), f32),
            pltpu.VMEM((2, rows + 16, 128), f32),
            pltpu.VMEM((2, rows + 16, 128), f32),
            pltpu.VMEM((2 * ITERS, 8, 128), f32),
            pltpu.VMEM((n_cols - 1, 1, 128), f32),
            pltpu.VMEM((n_rows - 1, 1, 128), f32),
            pltpu.VMEM((2, 1, 128), f32),
            pltpu.SemaphoreType.DMA((1 + (tiles - 2) // group_of(tiles) * -(-group_of(tiles) // PIECE),)),
            pltpu.SemaphoreType.DMA((2, 4)),
            pltpu.SemaphoreType.DMA((2, 2)),
        ],
        compiler_params=pltpu.CompilerParams(
            collective_id=0, has_side_effects=True, vmem_limit_bytes=20 * 2**20
        ),
    )(*arrays)
    made = [pltpu.with_memory_space_constraint(a, pltpu.VMEM) for a in made]
    blended, residual = pl.pallas_call(
        combine_kernel,
        out_shape=[jax.ShapeDtypeStruct(guidance.shape, f32)] * 2,
        in_specs=[vmem] * 6,
        out_specs=[hbm] * 2,
        scratch_shapes=[
            pltpu.VMEM((2, channels, rows, width), f32),
            pltpu.SemaphoreType.DMA((2,)),
        ],
        compiler_params=pltpu.CompilerParams(vmem_limit_bytes=12 * 2**20),
    )(*made)
    return blended, residual


def solution(mesh):
    s3, s2 = P(None, "rows", "cols"), P("rows", "cols")
    body = functools.partial(on_device, mesh.shape["rows"], mesh.shape["cols"])
    return jax.shard_map(
        body, mesh=mesh, in_specs=(s3, s3, s2, s2), out_specs=(s3, s3), check_vma=False
    )
```

```python
import functools

import jax
import jax.numpy as jnp
from jax import lax
from jax.experimental import pallas as pl
from jax.experimental.pallas import tpu as pltpu
from jax.sharding import PartitionSpec as P

ITERS = 3
CH = 3
SCREEN = 0.1
SEAM_WEIGHT = 0.5
SHIFT = 2.5
MESH = pl.DeviceIdType.MESH
RIM = ITERS + 1
GROUP = 11


def neighbours(ref, lead, tile, at, lane):
    col, before, after = tile
    here = ref[(*lead, col, pl.ds(at, 8), slice(None))]
    up = ref[(*lead, col, pl.ds(at - 1, 8), slice(None))]
    down = ref[(*lead, col, pl.ds(at + 1, 8), slice(None))]
    axis = here.ndim - 1
    left = ref[(*lead, before, pl.ds(at, 8), slice(None))]
    right = ref[(*lead, after, pl.ds(at, 8), slice(None))]
    left = pltpu.roll(jnp.where(lane == 127, left, here), 1, axis)
    right = pltpu.roll(jnp.where(lane == 0, right, here), 127, axis)
    return here, down, up, right, left


PIECE = 4


def group_of(tiles):
    return max(k for k in range(1, GROUP + 1) if (tiles - 2) % k == 0)


def krylov_kernel(
    guidance, initial, labels, dirichlet,
    x, u0, u1, u2, u3, coef,
    marks, fixed, weights, col_out, col_in, sums, gather_a, gather_b, mine,
    load_sem, rim_sem, sum_sem,
):
    n_rows, n_cols = lax.axis_size("rows"), lax.axis_size("cols")
    my_row, my_col = lax.axis_index("rows"), lax.axis_index("cols")
    rows, width = labels.shape
    tiles = width // 128
    fields = (u0, u1, u2, u3)
    given = u3
    group = group_of(tiles)
    groups = (tiles - 2) // group
    inside, middle = pl.ds(8, rows), pl.ds(1, tiles)

    row_peers = [lax.rem(my_row + k, n_rows) for k in range(1, n_rows)]
    col_peers = [lax.rem(my_col + k, n_cols) for k in range(1, n_cols)]
    row_up, row_down = row_peers[-1], row_peers[0]
    col_left, col_right = col_peers[-1], col_peers[0]
    diagonal_peers = [(r, c) for r in (row_up, row_down) for c in (col_left, col_right)]
    greeted = [(peer, my_col) for peer in row_peers] + [(my_row, peer) for peer in col_peers] + diagonal_peers
    barrier = pltpu.get_barrier_semaphore()
    for peer in greeted:
        pl.semaphore_signal(barrier, inc=1, device_id=peer, device_id_type=MESH)

    def load(tile, sem):
        columns = pl.ds(pl.multiple_of((tile - 1) * 128, 128), 128)
        pltpu.make_async_copy(initial.at[:, :, columns], x.at[:, tile, inside, :], sem).start()
        pltpu.make_async_copy(labels.at[:, columns], marks.at[tile, inside, :], sem).start()

    def load_other(tile, sem):
        columns = pl.ds(pl.multiple_of((tile - 1) * 128, 128), 128)
        pltpu.make_async_copy(guidance.at[:, :, columns], given.at[:, tile, inside, :], sem).start()
        pltpu.make_async_copy(dirichlet.at[:, columns], fixed.at[tile, inside, :], sem).start()

    pieces = [(1, 2)] + [(3 + k, min(PIECE, group - k)) for k in range(0, group, PIECE)]
    rest = tiles - 2 - group
    for index, (tile, count) in enumerate(pieces):

        @pl.loop(tile, tile + count)
        def _(tile):
            load(tile, load_sem.at[index])
            load_other(tile, load_sem.at[index])

    if rest:
        pl.loop(3 + group, tiles + 1)(lambda tile: load(tile, load_sem.at[len(pieces)]))
    later = [
        (3 + step * group + k, min(PIECE, group - k)) for step in range(1, groups) for k in range(0, group, PIECE)
    ]
    for index, (tile, count) in enumerate(later):

        @pl.loop(tile, tile + count)
        def _(tile):
            load_other(tile, load_sem.at[len(pieces) + 1 + index])

    lane8 = lax.broadcasted_iota(jnp.int32, (8, 128), 1)
    sub8 = lax.broadcasted_iota(jnp.int32, (8, 128), 0)
    lane24 = lax.broadcasted_iota(jnp.int32, (CH, 8, 128), 2)
    every = (slice(None),)

    def arrived(ref, sem):
        pltpu.make_async_copy(ref, ref, sem).wait()

    def loaded(index, size):
        arrived(weights.at[0:4, pl.ds(1, size), inside, :], load_sem.at[index])

    def remote(src, dst, send, recv, peer):
        return pltpu.make_async_remote_copy(
            src_ref=src, dst_ref=dst, send_sem=send, recv_sem=recv, device_id=peer, device_id_type=MESH
        )

    def rim_copies():
        copies = []
        for ref, size, lead in ((x, RIM, every), (marks, RIM, ()), (given, RIM - 1, every), (fixed, RIM - 1, ())):
            for way, peer in ((0, row_up), (1, row_down)):
                source, target = (8, 8 + rows) if way == 0 else (8 + rows - size, 8 - size)
                copies.append(
                    functools.partial(
                        remote,
                        ref.at[(*lead, middle, pl.ds(source, size), slice(None))],
                        ref.at[(*lead, middle, pl.ds(target, size), slice(None))],
                        rim_sem.at[0, way], rim_sem.at[1, way], (peer, my_col),
                    )
                )
        for side, peer in ((0, col_left), (1, col_right)):
            for r, source, target, size in (
                (my_row, 8, 8, rows),
                (row_up, 8, 8 + rows, RIM),
                (row_down, 8 + rows - RIM, 8 - RIM, RIM),
            ):
                copies.append(
                    functools.partial(
                        remote,
                        col_out.at[side, pl.ds(source, size)], col_in.at[side, pl.ds(target, size)],
                        rim_sem.at[0, 2 + side], rim_sem.at[1, 2 + side], (r, peer),
                    )
                )
        return copies

    def pack_columns():
        for side, tile, lane in ((0, 1, 0), (1, tiles, 128 - RIM)):
            for at in range(8, 8 + rows, 8):
                values = [ref[ch, tile, at : at + 8, :] for ref in (x, given) for ch in range(CH)]
                values += [ref[tile, at : at + 8, :].astype(jnp.float32) for ref in (marks, fixed)]
                packed = jnp.zeros((8, 128), jnp.float32)
                for index, value in enumerate(values):
                    packed = jnp.where(lane8 // RIM == index, pltpu.roll(value, (index * RIM - lane) % 128, 1), packed)
                col_out[side, at : at + 8, :] = packed

    def take_rim():
        sent = (CH + 1) * (2 * RIM - 1)
        for kind in (1, 0):
            for way in range(2):
                arrived(marks.at[middle, pl.ds(0, sent), :], rim_sem.at[kind, way])
                arrived(col_in.at[way, pl.ds(8 - RIM, rows + 2 * RIM)], rim_sem.at[kind, 2 + way])
        blank = jnp.where(lane8 // RIM == 2 * CH, -1.0, jnp.where(lane8 // RIM == 2 * CH + 1, 1.0, 0.0))
        not_first, not_last = my_row > 0, my_row < n_rows - 1
        for at in range(0, 16 + rows, 8):
            there = [my_col < n_cols - 1, my_col > 0]
            if at == 0:
                there = [jnp.logical_and(t, not_first) for t in there]
            if at == 8 + rows:
                there = [jnp.logical_and(t, not_last) for t in there]
            right, left = [jnp.where(t, col_in[side, at : at + 8, :], blank) for side, t in enumerate(there)]
            for index in range(2 * CH + 2):
                value = jnp.where(
                    lane8 < 64,
                    pltpu.roll(right, (128 - index * RIM) % 128, 1),
                    pltpu.roll(left, (128 - RIM - index * RIM) % 128, 1),
                )
                if index < 2 * CH:
                    (x, given)[index // CH][index % CH, 0, at : at + 8, :] = value
                else:
                    (marks, fixed)[index - 2 * CH][0, at : at + 8, :] = value.astype(jnp.int32)

        def clear(at):
            for k in range(1, tiles + 1):
                for ref in (x, given):
                    ref[:, k, at : at + 8, :] = jnp.zeros((CH, 8, 128), jnp.float32)
                marks[k, at : at + 8, :] = jnp.full((8, 128), -1, jnp.int32)
                fixed[k, at : at + 8, :] = jnp.ones((8, 128), jnp.int32)

        pl.when(my_row == 0)(lambda: clear(0))
        pl.when(my_row == n_rows - 1)(lambda: clear(8 + rows))

    def first(tile, at):
        col, here8 = tile[0], pl.ds(at, 8)
        mark, *sides = neighbours(marks, (), tile, at, lane8)
        free = (1 - fixed[col, here8, :]).astype(jnp.float32)
        whole, part = -free, -SEAM_WEIGHT * free
        negated = [jnp.where(side == mark, whole, part) for side in sides]
        diagonal = SCREEN * free - ((negated[0] + negated[1]) + (negated[2] + negated[3]))
        for index, value in enumerate([diagonal - SHIFT * free, *negated]):
            weights[index, col, here8, :] = value
        here, *sides = neighbours(x, every, tile, at, lane24)
        total = free * given[:, col, here8, :] - diagonal * here
        for weight, side in zip(negated, sides):
            total = total - weight * side
        u0[:, col, here8, :] = total
        return None, total

    def work(stage, tile, at):
        if stage == 0:
            return first(tile, at)
        col, here8 = tile[0], pl.ds(at, 8)
        here, *sides = neighbours(fields[stage - 1], every, tile, at, lane24)
        total = weights[0, col, here8, :] * here
        for index, side in enumerate(sides):
            total = total + weights[index + 1, col, here8, :] * side
        fields[stage][:, col, here8, :] = total
        return here, total

    def form(tile, at):
        col, _, after = tile
        here8 = pl.ds(at, 8)
        here = u2[:, col, here8, :]
        right = pltpu.roll(jnp.where(lane24 == 0, u2[:, after, here8, :], here), 127, 2)
        own = weights[0, col, here8, :] * here
        edges = weights[1, col, here8, :] * u2[:, col, pl.ds(at + 1, 8), :] + weights[3, col, here8, :] * right
        return here, here * own, here * edges

    def load_until(step, k):
        per_step = -(-group // PIECE)
        copies = rim_copies()
        if step == 0:
            loaded(1 + k // PIECE, 2 * pieces[1 + k // PIECE][1])
        else:
            if step == 1 and k == 0:
                loaded(len(pieces), rest)
                pl.semaphore_wait(barrier, len(greeted))
                for copy in copies[:4]:
                    copy().start()
            index = (step - 1) * per_step + k // PIECE
            loaded(len(pieces) + 1 + index, later[index][1])
        if step == groups - 1 and k + PIECE >= group:
            if step == 0:
                pl.semaphore_wait(barrier, len(greeted))
            for copy in copies[0 if step == 0 else 4 : 8]:
                copy().start()
            pack_columns()
            for copy in copies[8:]:
                copy().start()

    def add(acc, products):
        return tuple(a + p for a, p in zip(acc, products))

    def inner(stage):
        low, high = 9 + stage, 8 + rows - 9 - stage
        last = stage == ITERS

        def body(step, acc):
            for k in range(group):
                if stage == 0 and k % PIECE == 0:
                    load_until(step, k)
                col = 2 + step * group + k
                tile = (col, col - 1, col + 1)
                if not last:
                    work(stage, tile, low)
                for at in range(16, rows, 8):
                    if last:
                        acc = add(acc, form(tile, at)[1:])
                        continue
                    here, total = work(stage, tile, at)
                    acc = add(acc, [total * total] if stage == 0 else [here * total, total * total])
                if not last:
                    work(stage, tile, high)
            return acc

        acc = (jnp.zeros((CH, 8, 128), jnp.float32),) * (1 if stage == 0 else 2)
        if stage == 0:
            loaded(0, 2 * pieces[0][1])
            for step in range(groups):
                acc = body(step, acc)
        else:
            acc = lax.fori_loop(0, groups, body, acc)
        if not last:
            for tile in ((1, 1, 2), (tiles, tiles - 1, tiles)):
                for at in (low, *range(16, rows, 8), high):
                    work(stage, tile, at)
        return acc

    sides = [(1, 0, 2), (tiles, tiles - 1, 0)]

    def outer(stage):
        beyond = RIM - 1 - stage
        low, high = 8 - beyond, rows + beyond
        for col in range(2, tiles):
            for at in (low, high):
                work(stage, (col, col - 1, col + 1), at)
        for tile in (*sides, (0, tiles, 1)):
            for at in (low, *range(8, 8 + rows, 8), high):
                work(stage, tile, at)

    def outer_sums(acc):
        places = [((col, col - 1, col + 1), at) for col in range(2, tiles) for at in (8, rows)]
        places += [(tile, at) for tile in sides for at in range(8, 8 + rows, 8)]
        for tile, at in places:
            zero, one = [field[:, tile[0], pl.ds(at, 8), :] for field in (u0, u1)]
            two, own, edges = form(tile, at)
            acc = add(acc, [zero * zero, zero * one, one * one, one * two, two * two, own, edges])
        return acc

    def final_stage(part):
        def body(step, carry):
            for k in range(group):
                col = 2 + step * group + k
                for at in range(8, 8 + rows, 8):
                    work(ITERS, (col, col - 1, col + 1), at)
            return carry

        half = groups // 2
        lax.fori_loop(half * part, groups if part else half, body, 0)
        for at in range(8, 8 + rows, 8):
            work(ITERS, sides[part], at)

    moments = []
    for stage in range(ITERS + 1):
        moments.extend(inner(stage))
    take_rim()
    for stage in range(ITERS):
        outer(stage)
    *moments, own, edges = outer_sums(moments)
    moments.append(own + 2.0 * edges)

    message = jnp.zeros((8, 128), jnp.float32)
    for index, value in enumerate(moments):
        for ch in range(CH):
            sums[index, ch : ch + 1, :] = jnp.sum(value[ch], axis=0, keepdims=True)
        total = jnp.sum(jnp.where(sub8 < CH, sums[index], 0.0), axis=1, keepdims=True)
        message = jnp.where(lane8 == 8 * index + sub8, total, message)
    message = jnp.sum(message, axis=0, keepdims=True)

    total = message
    for part, (slots, targets) in enumerate(
        ((gather_a, [(my_row, peer) for peer in col_peers]), (gather_b, [(peer, my_col) for peer in row_peers]))
    ):
        mine[part] = total
        for k, target in enumerate(targets):
            remote(mine.at[part], slots.at[k], sum_sem.at[part, 0], sum_sem.at[part, 1], target).start()
        final_stage(part)
        arrived(slots, sum_sem.at[part, 1])
        arrived(slots, sum_sem.at[part, 0])
        parts = [total] + [slots[k] for k in range(len(targets))]
        while len(parts) > 1:
            parts = [functools.reduce(jnp.add, parts[i : i + 2]) for i in range(0, len(parts), 2)]
        total = parts[0]
    total = jnp.broadcast_to(total, (8, 128))
    m = [
        jnp.broadcast_to(jnp.sum(jnp.where(lane8 == 8 * k + sub8, total, 0.0), axis=1, keepdims=True), (8, 128))
        for k in range(2 * ITERS)
    ]

    def dot(p, q, moments):
        return functools.reduce(
            jnp.add, [a * b * moments[i + j] for i, a in enumerate(p) for j, b in enumerate(q)]
        )

    image = [m[k + 1] + SHIFT * m[k] for k in range(2 * ITERS - 1)]
    one = jnp.ones((8, 128), jnp.float32)
    residual, direction, blended = [one], [one], []
    norm_now = m[0]
    for turn in range(ITERS):
        step_size = norm_now / dot(direction, direction, image)
        blended = [
            (blended[i] if i < len(blended) else 0.0) + step_size * p for i, p in enumerate(direction)
        ]
        applied = [SHIFT * p for p in direction] + [jnp.zeros_like(one)]
        for i, p in enumerate(direction):
            applied[i + 1] = applied[i + 1] + p
        residual = [
            (residual[i] if i < len(residual) else 0.0) - step_size * a for i, a in enumerate(applied)
        ]
        if turn + 1 < ITERS:
            norm_next = dot(residual, residual, m)
            ratio = norm_next / norm_now
            direction = [
                r + (ratio * direction[i] if i < len(direction) else 0.0) for i, r in enumerate(residual)
            ]
            norm_now = norm_next
    for index, value in enumerate(blended + residual):
        coef[index] = value


def combine_kernel(x, u0, u1, u2, u3, coef, blended, residual, stage, sem):
    rows = blended.shape[1]
    tiles = blended.shape[2] // 128

    def out(which, ref, step):
        here = pl.ds(pl.multiple_of(step * 8, 8), 8)
        return pltpu.make_async_copy(stage.at[which, :, here], ref.at[:, here], sem.at[which])

    @pl.loop(0, rows // 8)
    def _(step):
        there = pl.ds(pl.multiple_of(step * 8, 8), 8)
        here = pl.ds(pl.multiple_of(8 + step * 8, 8), 8)
        for ch in range(CH):
            c = [coef[i, ch : ch + 1, :] for i in range(2 * ITERS + 1)]
            for tile in range(tiles):
                f = [u[ch, tile + 1, here, :] for u in (u0, u1, u2, u3)]
                iterate = x[ch, tile + 1, here, :] + c[0] * f[0] + c[1] * f[1] + c[2] * f[2]
                columns = slice(tile * 128, tile * 128 + 128)
                stage[0, ch, there, columns] = iterate
                stage[1, ch, there, columns] = (c[3] * f[0] + c[4] * f[1]) + (c[5] * f[2] + c[6] * f[3])
        out(0, blended, step).start()
        out(1, residual, step).start()

    for which, ref in enumerate((blended, residual)):
        pltpu.make_async_copy(stage.at[which], ref, sem.at[which]).wait()


def on_device(n_rows, n_cols, guidance, initial, labels, dirichlet):
    channels, rows, width = guidance.shape
    tiles = width // 128
    f32, i32 = jnp.float32, jnp.int32
    plane = (tiles + 1, rows + 16, 128)
    field = (channels, *plane)
    made_shape = pltpu.VMEM
    vmem, hbm = pl.BlockSpec(memory_space=pltpu.VMEM), pl.BlockSpec(memory_space=pltpu.HBM)
    arrays = [pltpu.with_memory_space_constraint(a, pltpu.HBM) for a in (guidance, initial, labels, dirichlet)]
    made = pl.pallas_call(
        krylov_kernel,
        out_shape=[made_shape(field, f32)] * 5 + [made_shape((2 * ITERS + 2, 8, 128), f32)],
        in_specs=[hbm] * 4,
        out_specs=[vmem] * 6,
        scratch_shapes=[
            pltpu.VMEM(plane, i32),
            pltpu.VMEM(plane, i32),
            pltpu.VMEM((5, *plane), f32),
            pltpu.VMEM((2, rows + 16, 128), f32),
            pltpu.VMEM((2, rows + 16, 128), f32),
            pltpu.VMEM((2 * ITERS, 8, 128), f32),
            pltpu.VMEM((n_cols - 1, 1, 128), f32),
            pltpu.VMEM((n_rows - 1, 1, 128), f32),
            pltpu.VMEM((2, 1, 128), f32),
            pltpu.SemaphoreType.DMA((2 + (tiles - 2) // group_of(tiles) * -(-group_of(tiles) // PIECE),)),
            pltpu.SemaphoreType.DMA((2, 4)),
            pltpu.SemaphoreType.DMA((2, 2)),
        ],
        compiler_params=pltpu.CompilerParams(
            collective_id=0, has_side_effects=True, vmem_limit_bytes=20 * 2**20
        ),
    )(*arrays)
    made = [pltpu.with_memory_space_constraint(a, pltpu.VMEM) for a in made]
    blended, residual = pl.pallas_call(
        combine_kernel,
        out_shape=[jax.ShapeDtypeStruct(guidance.shape, f32)] * 2,
        in_specs=[vmem] * 6,
        out_specs=[hbm] * 2,
        scratch_shapes=[
            pltpu.VMEM((2, channels, rows, width), f32),
            pltpu.SemaphoreType.DMA((2,)),
        ],
        compiler_params=pltpu.CompilerParams(vmem_limit_bytes=12 * 2**20),
    )(*made)
    return blended, residual


def solution(mesh):
    s3, s2 = P(None, "rows", "cols"), P("rows", "cols")
    body = functools.partial(on_device, mesh.shape["rows"], mesh.shape["cols"])
    return jax.shard_map(
        body, mesh=mesh, in_specs=(s3, s3, s2, s2), out_specs=(s3, s3), check_vma=False
    )
```
